512 devices in a mesh: lat: 64 (over y, z), lon: 8 (over x, core).
Axes of the slice: x: 4, y: 4, z: 16, core: 2. Of those that a mesh axis runs over, the one named last changes fastest.
Arguments:
- covariance: float32 [64, 64, 128, 128], P('lat', None, 'lon'), may hold values from -6 to 6
- winds: float32 [2, 3, 64, 128], P(None, None, None, 'lon'), may hold values from -0.35 to 0.35
- diffusivity: float32 [64, 128], P(None, 'lon'), may hold values from 0.01 to 0.07
- cutoff: int32 [64], replicated, may hold values from 4 to 16, as said below
Outputs:
- forecast: float32 [64, 64, 128, 128], P('lat', None, 'lon')
The draws below stay inside these ranges and needn't reach their ends.
Inputs may be any that keep to these rules, and one draw needn't show every extreme that they name: Some latitude has cutoff 16 and some other has 4.
All inputs are finite; a program needn't handle non-finite values.
Results may differ from the reference program's by a relative error of at most 0.00002.
Values sent between devices are 32-bit elements; how exact they have to be, the bound alone decides.
A program may use at most 192 MiB of HBM per device.

```python
import math
import jax
import jax.numpy as jnp
from jax import lax

STEPS = 3
NLAT = 64
NLON = 128
BAND = 16


def draw_cutoff(key, part):
    key_values, key_top, key_low = jax.random.split(key, 3)
    values = jax.random.randint(key_values, (NLAT,), BAND // 4, BAND + 1)
    top_at = jax.random.randint(key_top, (), 0, NLAT)
    low_at = (top_at + 1 + jax.random.randint(key_low, (), 0, NLAT - 1)) % NLAT
    places = jnp.arange(NLAT)
    values = jnp.where(places == top_at, BAND, values)
    values = jnp.where(places == low_at, BAND // 4, values)
    return values.astype(jnp.int32)


def block_levels(key, extent, pieces, low, high):
    level, own = 1.0, jax.random.fold_in(key, 6)
    for axis_at, blocks in pieces:
        heights = jnp.exp(jax.random.uniform(jax.random.fold_in(own, axis_at), (blocks,), jnp.float32, low / len(pieces), high / len(pieces)))
        level = level * jnp.repeat(heights, extent[axis_at] // blocks).reshape([-1 if axis == axis_at else 1 for axis in range(len(extent))])
    return level


def noise(stream_key, extent, width, most, pieces=(), kind=jnp.bfloat16):
    gain = block_levels(stream_key, extent, pieces, -0.22, 0.18) if pieces else 1.0
    result = jax.random.normal(stream_key, extent, jnp.float32) * width * gain
    return jnp.minimum(jnp.maximum(result, -most), most).astype(kind)


def setup_inputs(seed: int = 0) -> dict:
    seeds = jax.random.split(jax.random.key(seed), 5)
    return {
        "covariance": noise(seeds[0], (NLAT, NLAT, NLON, NLON), 1.0, 6.0, ((0, 64), (2, 8)), jnp.float32),
        "winds": jnp.clip(jax.random.uniform(seeds[1], (2, STEPS, NLAT, NLON), jnp.float32, -0.35, 0.35) * block_levels(seeds[1], (2, STEPS, NLAT, NLON), ((3, 8),), -0.4, 0.0), -0.35, 0.35),
        "diffusivity": jnp.clip(jnp.exp(math.log(0.07) - 1.9459102 * jax.random.uniform(seeds[2], (NLAT, NLON), jnp.float32) ** block_levels(seeds[2], (NLAT, NLON), ((1, 8),), -0.2, 0.2)), 0.01, 0.07),
        "cutoff": draw_cutoff(jax.random.fold_in(seeds[4], 71), 0),
    }


def advance(tracer, east_wind, north_wind, spread):
    western = jnp.roll(tracer, 1, axis=1)
    eastern = jnp.roll(tracer, -1, axis=1)
    zeros_row = jnp.zeros_like(tracer[:1])
    southern = jnp.concatenate([zeros_row, tracer[:-1]], axis=0)
    northern = jnp.concatenate([tracer[1:], zeros_row], axis=0)
    east_wind = east_wind[:, :, None]
    north_wind = north_wind[:, :, None]
    spread = spread[:, :, None]
    transport = (jnp.maximum(east_wind, 0.0) * (tracer - western)
                 + jnp.minimum(east_wind, 0.0) * (eastern - tracer)
                 + jnp.maximum(north_wind, 0.0) * (tracer - southern)
                 + jnp.minimum(north_wind, 0.0) * (northern - tracer))
    return tracer - transport + spread * (eastern + western + northern + southern - 4.0 * tracer)


def evolve(tracer, winds, diffusivity):
    for substep in range(STEPS):
        tracer = advance(tracer, winds[0, substep], winds[1, substep], diffusivity)
    return tracer


def reference(covariance, winds, diffusivity, cutoff):
    latitude = jnp.arange(NLAT, dtype=jnp.int32)
    keep_first = jnp.abs(latitude[None, :] - latitude[:, None]) <= cutoff[None, :]
    state_field = jnp.where(keep_first[:, :, None, None], covariance, 0.0)
    state_field = lax.map(lambda lat_row: evolve(lat_row, winds, diffusivity), state_field)
    state_field = jnp.transpose(state_field, (1, 0, 3, 2))
    state_field = lax.map(lambda lat_row: evolve(lat_row, winds, diffusivity), state_field)
    keep_second = jnp.abs(latitude[None, :] - latitude[:, None]) <= cutoff[:, None]
    state_field = jnp.where(keep_second[:, :, None, None], state_field, 0.0)
    return jnp.transpose(state_field, (1, 0, 3, 2))
```

```python
import functools

import jax
import jax.numpy as jnp
from jax import lax
from jax.experimental import pallas as pl
from jax.experimental.pallas import tpu as pltpu
from jax.sharding import PartitionSpec as P

MESH = pl.DeviceIdType.MESH
NLAT = 64
WIDE = 16
OFF = 20
ROWS = 2 * OFF + 1
B1 = (-17, -10, -3, 4, 11, 18)
B2 = (-17, -14, -7, 0, 7, 13, 18)
B3 = (-16, -15, -8, -1, 6, 12, 17)
HALO = 8


def pieces(bounds, low, high):
    return [(max(a, low), min(b, high + 1)) for a, b in zip(bounds[:-1], bounds[1:])]


def kernel(lats, lons, x_ref, winds_ref, diff_ref, cut_ref, out_ref,
           xv, xm, wv, dv, l1, r1, l2, r2, l3, r3, e0, e1, e2, h1, h2, co, tab, gath,
           load_sem, s_send, s_recv, p_send, p_recv, t_send, t_recv, g_send, g_recv):
    j = lax.axis_index("lat")
    b = lax.axis_index("lon")
    up, down = lax.rem(j + 1, lats), lax.rem(j + lats - 1, lats)
    east, west = lax.rem(b + 1, lons), lax.rem(b + lons - 1, lons)

    barrier = pltpu.get_barrier_semaphore()
    pl.semaphore_signal(barrier, inc=1, device_id=(up, b), device_id_type=MESH)
    pl.semaphore_signal(barrier, inc=1, device_id=(down, b), device_id_type=MESH)
    for d in range(1, lons):
        pl.semaphore_signal(barrier, inc=1, device_id=(j, lax.rem(b + d, lons)), device_id_type=MESH)

    load_x = pltpu.make_async_copy(x_ref.at[0], xv, load_sem.at[0])
    load_w = pltpu.make_async_copy(winds_ref, wv, load_sem.at[1])
    load_d = pltpu.make_async_copy(diff_ref, dv, load_sem.at[2])
    load_x.start()
    load_w.start()
    load_d.start()

    def lat_of(n):
        return lax.rem(j + n + (NLAT - OFF), NLAT)

    def keep(n):
        cut = cut_ref[lat_of(n)]
        inside = jnp.logical_and(j + n >= OFF, j + n < NLAT + OFF)
        near = jnp.logical_and(n <= OFF + cut, n + cut >= OFF)
        return jnp.where(jnp.logical_and(inside, near), 1.0, 0.0).astype(jnp.float32)

    zero = jnp.zeros((16, 128), jnp.float32)
    zero_e = jnp.zeros((2 * HALO + 16, 128), jnp.float32)
    for r in (-17, 17):
        xm[r + OFF] = zero
    for r in (16, 17):
        l1[r + OFF] = zero
        r1[-r + OFF] = zero
    for r in (18, 19, 20):
        e0[r + OFF] = zero_e
        e0[-r + OFF] = zero_e
    for r in (19, 20):
        e1[r + OFF] = zero_e
        e1[-r + OFF] = zero_e

    load_x.wait()

    @pl.loop(OFF - WIDE, OFF + WIDE + 1)
    def _(n):
        xm[n] = xv[lat_of(n)] * keep(n)

    pl.semaphore_wait(barrier, 2 + lons - 1)

    def exchange(level, bounds, index, source, from_down, from_up, low, high):
        a, e = pieces(bounds, low, high)[index]
        to_up = pltpu.make_async_remote_copy(
            source.at[pl.ds(a + 1 + OFF, e - a)], from_down.at[pl.ds(a + OFF, e - a)],
            s_send.at[level, 0, index], s_recv.at[level, 0, index], device_id=(up, b), device_id_type=MESH)
        a, e = pieces(bounds, -high, -low)[index]
        to_down = pltpu.make_async_remote_copy(
            source.at[pl.ds(a - 1 + OFF, e - a)], from_up.at[pl.ds(a + OFF, e - a)],
            s_send.at[level, 1, index], s_recv.at[level, 1, index], device_id=(down, b), device_id_type=MESH)
        return to_up, to_down

    level1 = [exchange(0, B1, n, xm, l1, r1, -17, 15) for n in range(len(B1) - 1)]
    level2 = [exchange(1, B2, n, h1, l2, r2, -17, 17) for n in range(len(B2) - 1)]
    level3 = [exchange(2, B3, n, h2, l3, r3, -16, 16) for n in range(len(B3) - 1)]

    def begin(copies):
        for copy in copies:
            copy.start()

    for copies in level1:
        begin(copies)

    load_w.wait()
    load_d.wait()
    fields = [wv.at[c, s] for c in range(2) for s in range(3)] + [dv]
    lane = lax.broadcasted_iota(jnp.int32, (NLAT, 128), 1)
    sub = lax.broadcasted_iota(jnp.int32, (NLAT, 128), 0)
    turn = jnp.where(lane == sub - j + OFF, 1.0, 0.0).astype(jnp.float32)
    lane = lax.broadcasted_iota(jnp.int32, (16, 128), 1)
    sub = lax.broadcasted_iota(jnp.int32, (16, 128), 0)
    place = jnp.where(lane == sub + b * 16, 1.0, 0.0).astype(jnp.float32)
    mine = []
    for n, f in enumerate(fields):
        table = jnp.dot(f[...], turn, precision=lax.Precision.HIGHEST, preferred_element_type=jnp.float32)
        tab[n, HALO:HALO + 16, :] = table
        mine.append(jnp.sum(table[:, OFF:OFF + 1] * place, axis=0, keepdims=True))
    mine.append(jnp.zeros((1, 128), jnp.float32))
    gath[b] = jnp.concatenate(mine, axis=0)
    gathers = []
    for d in range(1, lons):
        copy = pltpu.make_async_remote_copy(
            gath.at[b], gath.at[b], g_send.at[d - 1], g_recv.at[d - 1],
            device_id=(j, lax.rem(b + d, lons)), device_id_type=MESH)
        copy.start()
        gathers.append(copy)

    lo, hi = pl.ds(0, HALO), pl.ds(HALO + 16, HALO)
    first, last = pl.ds(HALO, HALO), pl.ds(16, HALO)

    def halo(ref, send, recv, rows=None):
        rows = slice(None) if rows is None else rows
        to_east = pltpu.make_async_remote_copy(
            ref.at[rows, last], ref.at[rows, lo], send.at[0], recv.at[0],
            device_id=(j, east), device_id_type=MESH)
        to_west = pltpu.make_async_remote_copy(
            ref.at[rows, first], ref.at[rows, hi], send.at[1], recv.at[1],
            device_id=(j, west), device_id_type=MESH)
        return to_east, to_west

    tables = halo(tab, t_send, t_recv)
    begin(tables)

    @pl.loop(OFF + WIDE + 1, OFF + NLAT - WIDE)
    def _(n):
        out_ref[0, lat_of(n)] = zero

    for copy in gathers:
        copy.wait_recv()
    whole = gath[0]
    for d in range(1, lons):
        whole = whole + gath[d]
    k = whole[6:7]
    open_down = jnp.where(j == 0, 0.0, 1.0).astype(jnp.float32)
    open_up = jnp.where(j == NLAT - 1, 0.0, 1.0).astype(jnp.float32)

    def second(step, center, lower, upper):
        u, v = whole[step:step + 1], whole[3 + step:4 + step]
        c_w, c_e = k + jnp.maximum(u, 0.0), k - jnp.minimum(u, 0.0)
        c_s, c_n = k + jnp.maximum(v, 0.0), k - jnp.minimum(v, 0.0)
        c_0 = 1.0 - (c_w + c_e) - (c_s + c_n)
        c_s, c_n = c_s * open_down, c_n * open_up
        return (c_0 * center + c_w * pltpu.roll(center, 1, 1) + c_e * pltpu.roll(center, 127, 1)
                + c_s * lower + c_n * upper)

    def loop(a, e, body):
        def run(n, carry):
            body(n)
            return carry
        lax.fori_loop(a + OFF, e + OFF, run, 0)

    def do_g1(index):
        for copy in level1[index]:
            copy.wait_recv()
        a, e = B1[index], B1[index + 1]

        def body(n):
            e0[n, HALO:HALO + 16, :] = second(0, xm[n], l1[n], r1[n])
        loop(a, e, body)
        begin(halos[index])

    halos = [halo(e0, p_send.at[n], p_recv.at[n], pl.ds(B1[n] + OFF, B1[n + 1] - B1[n])) for n in range(len(B1) - 1)]

    def do_coefficients(a, e):
        for r in range(a, e):
            at = slice(r + OFF, r + OFF + 1)
            k_r = jnp.broadcast_to(tab[6, :, at], zero_e.shape)
            for s in range(3):
                u = jnp.broadcast_to(tab[s, :, at], zero_e.shape)
                v = jnp.broadcast_to(tab[3 + s, :, at], zero_e.shape)
                c_w, c_e = k_r + jnp.maximum(u, 0.0), k_r - jnp.minimum(u, 0.0)
                c_s, c_n = k_r + jnp.maximum(v, 0.0), k_r - jnp.minimum(v, 0.0)
                co[s, 0, r + OFF] = 1.0 - (c_w + c_e) - (c_s + c_n)
                co[s, 1, r + OFF] = c_w
                co[s, 2, r + OFF] = c_e
                co[s, 3, r + OFF] = c_s
                co[s, 4, r + OFF] = c_n

    def first_step(step, source, store, a, e):
        def body(n):
            center = source[n]
            store(n, co[step, 0, n] * center + co[step, 1, n] * pltpu.roll(center, 1, 0)
                  + co[step, 2, n] * pltpu.roll(center, 2 * HALO + 15, 0)
                  + co[step, 3, n] * source[n - 1] + co[step, 4, n] * source[n + 1])
        loop(a, e, body)

    def store_1(n, value):
        e1[n] = value

    def store_2(n, value):
        e2[n] = value

    def store_3(n, value):
        h1[n] = value[HALO:HALO + 16]

    done = [-18, -19, -18]

    def do_a1(end):
        for step, (source, store, limit, ahead) in enumerate(
                ((e0, store_1, 19, 2), (e1, store_2, 20, 1), (e2, store_3, 19, 0))):
            stop = min(end + ahead, limit)
            first_step(step, source, store, done[step], stop)
            done[step] = stop

    def do_h2(index):
        for copy in level2[index]:
            copy.wait_recv()

        def body(n):
            h2[n] = second(1, h1[n], l2[n], r2[n])
        loop(B2[index], B2[index + 1], body)

    def do_out(index):
        for copy in level3[index]:
            copy.wait_recv()

        def body(n):
            out_ref[0, lat_of(n)] = second(2, h2[n], l3[n], r3[n]) * keep(n)
        loop(B3[index], B3[index + 1], body)

    def wait_halo(index):
        for copy in halos[index]:
            copy.wait_recv()

    do_g1(0)
    for copy in tables:
        copy.wait_recv()
    do_coefficients(-19, 0)
    do_g1(1)
    do_coefficients(0, 20)

    def a1_for(index):
        do_a1(B2[index + 1] + 1)
        begin(level2[index])

    wait_halo(0)
    a1_for(0)
    do_g1(2)
    wait_halo(1)
    a1_for(1)
    do_g1(3)
    wait_halo(2)
    a1_for(2)
    do_g1(4)
    wait_halo(3)
    a1_for(3)
    wait_halo(4)
    a1_for(4)
    a1_for(5)
    for n in range(len(B2) - 1):
        do_h2(n)
        begin(level3[n])
    for n in range(len(B3) - 1):
        do_out(n)

    for copies in level1 + level2 + level3 + halos + [tables] + [gathers]:
        for copy in copies:
            copy.wait_send()


def per_device(covariance, winds, diffusivity, cutoff):
    lats, lons = lax.axis_size("lat"), lax.axis_size("lon")
    vm = lambda *shape: pltpu.VMEM(shape, jnp.float32)
    dma = lambda *shape: pltpu.SemaphoreType.DMA(shape)
    block = (ROWS, 16, 128)
    ext = (ROWS, 16 + 2 * HALO, 128)
    most = max(len(B1), len(B2), len(B3)) - 1
    return pl.pallas_call(
        functools.partial(kernel, lats, lons),
        out_shape=jax.ShapeDtypeStruct(covariance.shape, jnp.float32),
        in_specs=[pl.BlockSpec(memory_space=pl.ANY)] * 3 + [pl.BlockSpec(memory_space=pltpu.SMEM)],
        out_specs=pl.BlockSpec(memory_space=pltpu.VMEM),
        scratch_shapes=[
            vm(NLAT, 16, 128), vm(*block), vm(2, 3, 16, NLAT), vm(16, NLAT),
            vm(*block), vm(*block), vm(*block), vm(*block), vm(*block), vm(*block),
            vm(*ext), vm(*ext), vm(*ext), vm(*block), vm(*block),
            vm(3, 5, *ext), vm(7, 16 + 2 * HALO, 128), vm(lons, 8, 128),
            dma(3), dma(3, 2, most), dma(3, 2, most), dma(len(B1) - 1, 2), dma(len(B1) - 1, 2),
            dma(2), dma(2), dma(lons - 1), dma(lons - 1),
        ],
        compiler_params=pltpu.CompilerParams(
            collective_id=0, has_side_effects=True, vmem_limit_bytes=40 * 1024 * 1024),
        cost_estimate=pl.CostEstimate(flops=20_000_000, bytes_accessed=1_500_000, transcendentals=0),
    )(covariance, jnp.transpose(winds, (0, 1, 3, 2)), jnp.transpose(diffusivity), cutoff)


def solution(mesh):
    in_specs = (P("lat", None, "lon", None), P(None, None, None, "lon"), P(None, "lon"), P())
    out_specs = P("lat", None, "lon", None)
    return jax.shard_map(
        per_device, mesh=mesh, in_specs=in_specs, out_specs=out_specs, check_vma=False
    )
```

```python
import functools

import jax
import jax.numpy as jnp
from jax import lax
from jax.experimental import pallas as pl
from jax.experimental.pallas import tpu as pltpu
from jax.sharding import PartitionSpec as P

MESH = pl.DeviceIdType.MESH
NLAT = 64
WIDE = 16
OFF = 20
ROWS = 2 * OFF + 1
B1 = (-17, -10, -3, 4, 11, 18)
B2 = (-17, -14, -7, 0, 7, 13, 18)
B3 = (-16, -15, -8, -1, 6, 12, 17)
HALO = 8


def pieces(bounds, low, high):
    return [(max(a, low), min(b, high + 1)) for a, b in zip(bounds[:-1], bounds[1:])]


def kernel(lats, lons, x_ref, winds_ref, diff_ref, cutoff_ref, out_ref,
           cut_ref, xv, xm, wv, dv, l1, r1, l2, r2, l3, r3, e0, e1, e2, h1, h2, co, tab, gath,
           load_sem, s_send, s_recv, p_send, p_recv, t_send, t_recv, g_send, g_recv):
    j = lax.axis_index("lat")
    b = lax.axis_index("lon")
    up, down = lax.rem(j + 1, lats), lax.rem(j + lats - 1, lats)
    has_up, has_down = j < lats - 1, j > 0
    east, west = lax.rem(b + 1, lons), lax.rem(b + lons - 1, lons)

    barrier = pltpu.get_barrier_semaphore()
    @pl.when(has_up)
    def _():
        pl.semaphore_signal(barrier, inc=1, device_id=(up, b), device_id_type=MESH)

    @pl.when(has_down)
    def _():
        pl.semaphore_signal(barrier, inc=1, device_id=(down, b), device_id_type=MESH)

    for d in range(1, lons):
        pl.semaphore_signal(barrier, inc=1, device_id=(j, lax.rem(b + d, lons)), device_id_type=MESH)

    load_x = pltpu.make_async_copy(x_ref.at[0], xv, load_sem.at[0])
    load_w = pltpu.make_async_copy(winds_ref, wv, load_sem.at[1])
    load_d = pltpu.make_async_copy(diff_ref, dv, load_sem.at[2])
    load_c = pltpu.make_async_copy(cutoff_ref, cut_ref, load_sem.at[3])
    load_x.start()
    load_c.start()
    load_w.start()
    load_d.start()

    def lat_of(n):
        return lax.rem(j + n + (NLAT - OFF), NLAT)

    def keep(n):
        cut = cut_ref[lat_of(n)]
        inside = jnp.logical_and(j + n >= OFF, j + n < NLAT + OFF)
        near = jnp.logical_and(n <= OFF + cut, n + cut >= OFF)
        return jnp.where(jnp.logical_and(inside, near), 1.0, 0.0).astype(jnp.float32)

    zero = jnp.zeros((16, 128), jnp.float32)
    zero_e = jnp.zeros((2 * HALO + 16, 128), jnp.float32)
    for r in (-17, 17):
        xm[r + OFF] = zero
    for r in (16, 17):
        l1[r + OFF] = zero
        r1[-r + OFF] = zero
    for r in (18, 19, 20):
        e0[r + OFF] = zero_e
        e0[-r + OFF] = zero_e
    for r in (19, 20):
        e1[r + OFF] = zero_e
        e1[-r + OFF] = zero_e

    for there, received in ((has_down, (l1, l2, l3)), (has_up, (r1, r2, r3))):
        @pl.when(jnp.logical_not(there))
        def _():
            @pl.loop(OFF - 18, OFF + 19)
            def _(n):
                for ref in received:
                    ref[n] = zero

    load_c.wait()
    load_x.wait()

    @pl.loop(OFF - WIDE, OFF + WIDE + 1)
    def _(n):
        xm[n] = xv[lat_of(n)] * keep(n)

    load_w.wait()
    load_d.wait()
    fields = [wv.at[c, s] for c in range(2) for s in range(3)] + [dv]
    lane = lax.broadcasted_iota(jnp.int32, (NLAT, 128), 1)
    sub = lax.broadcasted_iota(jnp.int32, (NLAT, 128), 0)
    turn = jnp.where(lane == sub - j + OFF, 1.0, 0.0).astype(jnp.float32)
    lane = lax.broadcasted_iota(jnp.int32, (16, 128), 1)
    sub = lax.broadcasted_iota(jnp.int32, (16, 128), 0)
    place = jnp.where(lane == sub + b * 16, 1.0, 0.0).astype(jnp.float32)
    mine = []
    for n, f in enumerate(fields):
        table = jnp.dot(f[...], turn, precision=lax.Precision.HIGHEST, preferred_element_type=jnp.float32)
        tab[n, HALO:HALO + 16, :] = table
        mine.append(jnp.sum(table[:, OFF:OFF + 1] * place, axis=0, keepdims=True))
    mine.append(jnp.zeros((1, 128), jnp.float32))
    gath[b] = jnp.concatenate(mine, axis=0)

    inner = jnp.logical_and(has_up, has_down)

    @pl.when(inner)
    def _():
        pl.semaphore_wait(barrier, lons + 1)

    @pl.when(jnp.logical_not(inner))
    def _():
        pl.semaphore_wait(barrier, lons)

    def exchange(level, bounds, index, source, from_down, from_up, low, high):
        a, e = pieces(bounds, low, high)[index]
        to_up = pltpu.make_async_remote_copy(
            source.at[pl.ds(a + 1 + OFF, e - a)], from_down.at[pl.ds(a + OFF, e - a)],
            s_send.at[level, 0, index], s_recv.at[level, 0, index], device_id=(up, b), device_id_type=MESH)
        a, e = pieces(bounds, -high, -low)[index]
        to_down = pltpu.make_async_remote_copy(
            source.at[pl.ds(a - 1 + OFF, e - a)], from_up.at[pl.ds(a + OFF, e - a)],
            s_send.at[level, 1, index], s_recv.at[level, 1, index], device_id=(down, b), device_id_type=MESH)
        return to_up, to_down

    level1 = [exchange(0, B1, n, xm, l1, r1, -17, 15) for n in range(len(B1) - 1)]
    level2 = [exchange(1, B2, n, h1, l2, r2, -17, 17) for n in range(len(B2) - 1)]
    level3 = [exchange(2, B3, n, h2, l3, r3, -16, 16) for n in range(len(B3) - 1)]

    def begin(copies):
        for copy in copies:
            copy.start()

    def send(pair):
        for there, copy in zip((has_up, has_down), pair):
            @pl.when(there)
            def _():
                copy.start()

    def receive(pair):
        for there, copy in zip((has_down, has_up), pair):
            @pl.when(there)
            def _():
                copy.wait_recv()

    send(level1[0])

    lo, hi = pl.ds(0, HALO), pl.ds(HALO + 16, HALO)
    first, last = pl.ds(HALO, HALO), pl.ds(16, HALO)

    def halo(ref, send, recv, rows=None):
        rows = slice(None) if rows is None else rows
        to_east = pltpu.make_async_remote_copy(
            ref.at[rows, last], ref.at[rows, lo], send.at[0], recv.at[0],
            device_id=(j, east), device_id_type=MESH)
        to_west = pltpu.make_async_remote_copy(
            ref.at[rows, first], ref.at[rows, hi], send.at[1], recv.at[1],
            device_id=(j, west), device_id_type=MESH)
        return to_east, to_west

    tables = halo(tab, t_send, t_recv)
    begin(tables)
    gathers = []
    for d in range(1, lons):
        copy = pltpu.make_async_remote_copy(
            gath.at[b], gath.at[b], g_send.at[d - 1], g_recv.at[d - 1],
            device_id=(j, lax.rem(b + d, lons)), device_id_type=MESH)
        copy.start()
        gathers.append(copy)
    send(level1[1])
    send(level1[2])

    @pl.loop(OFF + WIDE + 1, OFF + NLAT - WIDE)
    def _(n):
        out_ref[0, lat_of(n)] = zero

    for copy in gathers:
        copy.wait_recv()
    whole = gath[0]
    for d in range(1, lons):
        whole = whole + gath[d]
    k = whole[6:7]

    def second(step, center, lower, upper):
        u, v = whole[step:step + 1], whole[3 + step:4 + step]
        c_w, c_e = k + jnp.maximum(u, 0.0), k - jnp.minimum(u, 0.0)
        c_s, c_n = k + jnp.maximum(v, 0.0), k - jnp.minimum(v, 0.0)
        c_0 = 1.0 - (c_w + c_e) - (c_s + c_n)
        return (c_0 * center + c_w * pltpu.roll(center, 1, 1) + c_e * pltpu.roll(center, 127, 1)
                + c_s * lower + c_n * upper)

    def loop(a, e, body):
        def run(n, carry):
            body(n)
            return carry
        lax.fori_loop(a + OFF, e + OFF, run, 0)

    def do_g1(index):
        receive(level1[index])
        if index + 3 < len(level1):
            send(level1[index + 3])
        a, e = B1[index], B1[index + 1]

        def body(n):
            e0[n, HALO:HALO + 16, :] = second(0, xm[n], l1[n], r1[n])
        loop(a, e, body)
        begin(halos[index])

    halos = [halo(e0, p_send.at[n], p_recv.at[n], pl.ds(B1[n] + OFF, B1[n + 1] - B1[n])) for n in range(len(B1) - 1)]

    def do_coefficients(a, e):
        for r in range(a, e):
            at = slice(r + OFF, r + OFF + 1)
            k_r = jnp.broadcast_to(tab[6, :, at], zero_e.shape)
            for s in range(3):
                u = jnp.broadcast_to(tab[s, :, at], zero_e.shape)
                v = jnp.broadcast_to(tab[3 + s, :, at], zero_e.shape)
                c_w, c_e = k_r + jnp.maximum(u, 0.0), k_r - jnp.minimum(u, 0.0)
                c_s, c_n = k_r + jnp.maximum(v, 0.0), k_r - jnp.minimum(v, 0.0)
                co[s, 0, r + OFF] = 1.0 - (c_w + c_e) - (c_s + c_n)
                co[s, 1, r + OFF] = c_w
                co[s, 2, r + OFF] = c_e
                co[s, 3, r + OFF] = c_s
                co[s, 4, r + OFF] = c_n

    def first_step(step, source, store, a, e):
        def body(n):
            center = source[n]
            store(n, co[step, 0, n] * center + co[step, 1, n] * pltpu.roll(center, 1, 0)
                  + co[step, 2, n] * pltpu.roll(center, 2 * HALO + 15, 0)
                  + co[step, 3, n] * source[n - 1] + co[step, 4, n] * source[n + 1])
        loop(a, e, body)

    def store_1(n, value):
        e1[n] = value

    def store_2(n, value):
        e2[n] = value

    def store_3(n, value):
        h1[n] = value[HALO:HALO + 16]

    done = [-18, -19, -18]

    def do_a1(end):
        for step, (source, store, limit, ahead) in enumerate(
                ((e0, store_1, 19, 2), (e1, store_2, 20, 1), (e2, store_3, 19, 0))):
            stop = min(end + ahead, limit)
            first_step(step, source, store, done[step], stop)
            done[step] = stop

    def do_h2(index):
        receive(level2[index])

        def body(n):
            h2[n] = second(1, h1[n], l2[n], r2[n])
        loop(B2[index], B2[index + 1], body)

    def do_out(index):
        receive(level3[index])

        def body(n):
            out_ref[0, lat_of(n)] = second(2, h2[n], l3[n], r3[n]) * keep(n)
        loop(B3[index], B3[index + 1], body)

    def wait_halo(index):
        for copy in halos[index]:
            copy.wait_recv()

    do_g1(0)
    for copy in tables:
        copy.wait_recv()
    do_coefficients(-19, 0)
    do_g1(1)
    do_coefficients(0, 20)

    def a1_for(index):
        do_a1(B2[index + 1] + 1)
        send(level2[index])

    wait_halo(0)
    a1_for(0)
    do_g1(2)
    wait_halo(1)
    a1_for(1)
    do_g1(3)
    wait_halo(2)
    a1_for(2)
    do_g1(4)
    wait_halo(3)
    a1_for(3)
    wait_halo(4)
    a1_for(4)
    a1_for(5)
    for n in range(len(B2) - 1):
        do_h2(n)
        send(level3[n])
    for n in range(len(B3) - 1):
        do_out(n)

    for pair in level1 + level2 + level3:
        for there, copy in zip((has_up, has_down), pair):
            @pl.when(there)
            def _():
                copy.wait_send()
    for copies in halos + [tables] + [gathers]:
        for copy in copies:
            copy.wait_send()


def per_device(covariance, winds, diffusivity, cutoff):
    lats, lons = lax.axis_size("lat"), lax.axis_size("lon")
    vm = lambda *shape: pltpu.VMEM(shape, jnp.float32)
    dma = lambda *shape: pltpu.SemaphoreType.DMA(shape)
    block = (ROWS, 16, 128)
    ext = (ROWS, 16 + 2 * HALO, 128)
    most = max(len(B1), len(B2), len(B3)) - 1
    return pl.pallas_call(
        functools.partial(kernel, lats, lons),
        out_shape=jax.ShapeDtypeStruct(covariance.shape, jnp.float32),
        in_specs=[pl.BlockSpec(memory_space=pltpu.HBM)] * 4,
        out_specs=pl.BlockSpec(memory_space=pltpu.VMEM),
        scratch_shapes=[
            pltpu.SMEM((NLAT,), jnp.int32), vm(NLAT, 16, 128), vm(*block), vm(2, 3, 16, NLAT), vm(16, NLAT),
            vm(*block), vm(*block), vm(*block), vm(*block), vm(*block), vm(*block),
            vm(*ext), vm(*ext), vm(*ext), vm(*block), vm(*block),
            vm(3, 5, *ext), vm(7, 16 + 2 * HALO, 128), vm(lons, 8, 128),
            dma(4), dma(3, 2, most), dma(3, 2, most), dma(len(B1) - 1, 2), dma(len(B1) - 1, 2),
            dma(2), dma(2), dma(lons - 1), dma(lons - 1),
        ],
        compiler_params=pltpu.CompilerParams(
            collective_id=0, has_side_effects=True, vmem_limit_bytes=40 * 1024 * 1024),
        cost_estimate=pl.CostEstimate(flops=20_000_000, bytes_accessed=1_500_000, transcendentals=0),
    )(*(pltpu.with_memory_space_constraint(a, pltpu.HBM) for a in (
        covariance, jnp.transpose(winds, (0, 1, 3, 2)), jnp.transpose(diffusivity), cutoff)))


def solution(mesh):
    in_specs = (P("lat", None, "lon", None), P(None, None, None, "lon"), P(None, "lon"), P())
    out_specs = P("lat", None, "lon", None)
    return jax.shard_map(
        per_device, mesh=mesh, in_specs=in_specs, out_specs=out_specs, check_vma=False
    )
```

```python
import functools

import jax
import jax.numpy as jnp
from jax import lax
from jax.experimental import pallas as pl
from jax.experimental.pallas import tpu as pltpu
from jax.sharding import PartitionSpec as P

MESH = pl.DeviceIdType.MESH
NLAT = 64
WIDE = 16
REACH = 3
OFF = 22
ROWS = 2 * OFF + 1
HALO = 8
BOUNDS = (-19, -10, -1, 8, 14, 20)
PIECES = len(BOUNDS) - 1
NEEDED = ([(f, t) for f in (0, 3, 6) for t in range(-2, 3)] + [(f, t) for f in (1, 4) for t in range(-1, 2)]
          + [(2, 0), (5, 0)])
PACKED = 24


def piece(index, sign):
    low = max(BOUNDS[index] + sign * REACH, -WIDE)
    high = min(BOUNDS[index + 1] + sign * REACH, WIDE + 1)
    return (low, high) if high > low else None


def kernel(lats, lons, x_ref, winds_ref, diff_ref, cutoff_ref, out_ref,
           cut_ref, xv, xm, wv, dv, l1, r1, l2, r2, l3, r3, e0, e1, e2, co, tab, gath, taps,
           load_sem, s_send, s_recv, p_send, p_recv, t_send, t_recv, g_send, g_recv):
    j = lax.axis_index("lat")
    b = lax.axis_index("lon")
    up, down = lax.rem(j + 1, lats), lax.rem(j + lats - 1, lats)
    east, west = lax.rem(b + 1, lons), lax.rem(b + lons - 1, lons)
    has_up, has_down = j < lats - 1, j > 0

    barrier = pltpu.get_barrier_semaphore()

    @pl.when(has_up)
    def _():
        pl.semaphore_signal(barrier, inc=1, device_id=(up, b), device_id_type=MESH)

    @pl.when(has_down)
    def _():
        pl.semaphore_signal(barrier, inc=1, device_id=(down, b), device_id_type=MESH)

    for d in range(1, lons):
        pl.semaphore_signal(barrier, inc=1, device_id=(j, lax.rem(b + d, lons)), device_id_type=MESH)

    load_x = pltpu.make_async_copy(x_ref.at[0], xv, load_sem.at[0])
    load_w = pltpu.make_async_copy(winds_ref, wv, load_sem.at[1])
    load_d = pltpu.make_async_copy(diff_ref, dv, load_sem.at[2])
    load_c = pltpu.make_async_copy(cutoff_ref, cut_ref, load_sem.at[3])
    load_x.start()
    load_c.start()
    load_w.start()
    load_d.start()

    def lat_of(n):
        return lax.rem(j + n + (NLAT - OFF), NLAT)

    def keep(n):
        cut = cut_ref[lat_of(n)]
        inside = jnp.logical_and(j + n >= OFF, j + n < NLAT + OFF)
        near = jnp.logical_and(n <= OFF + cut, n + cut >= OFF)
        return jnp.where(jnp.logical_and(inside, near), 1.0, 0.0).astype(jnp.float32)

    zero = jnp.zeros((16, 128), jnp.float32)
    wide_shape = (2 * HALO + 16, 128)

    load_c.wait()
    load_x.wait()

    @pl.loop(OFF - WIDE, OFF + WIDE + 1)
    def _(n):
        xm[n] = xv[lat_of(n)] * keep(n)

    load_w.wait()
    load_d.wait()
    fields = [wv.at[c, s] for c in range(2) for s in range(3)] + [dv]
    lane = lax.broadcasted_iota(jnp.int32, (NLAT, 128), 1)
    sub = lax.broadcasted_iota(jnp.int32, (NLAT, 128), 0)
    turn = jnp.where(lane == sub - j + OFF, 1.0, 0.0).astype(jnp.float32)
    lane = lax.broadcasted_iota(jnp.int32, (16, 128), 1)
    sub = lax.broadcasted_iota(jnp.int32, (16, 128), 0)
    place = jnp.where(lane == sub + b * 16, 1.0, 0.0).astype(jnp.float32)
    tables_own = []
    for n, f in enumerate(fields):
        table = jnp.dot(f[...], turn, precision=lax.Precision.HIGHEST, preferred_element_type=jnp.float32)
        tab[n, HALO:HALO + 16, :] = table
        tables_own.append(table)
    mine = [jnp.sum(tables_own[f][:, OFF + t:OFF + t + 1] * place, axis=0, keepdims=True) for f, t in NEEDED]
    mine += [jnp.zeros((1, 128), jnp.float32)] * (PACKED - len(mine))
    gath[b] = jnp.concatenate(mine, axis=0)

    inner = jnp.logical_and(has_up, has_down)

    @pl.when(inner)
    def _():
        pl.semaphore_wait(barrier, lons + 1)

    @pl.when(jnp.logical_not(inner))
    def _():
        pl.semaphore_wait(barrier, lons)

    below, above = (xm, l1, l2, l3), (xm, r1, r2, r3)

    def hop(level, index, sign):
        rows = piece(index, sign)
        if rows is None:
            return None
        at = pl.ds(rows[0] + OFF, rows[1] - rows[0])
        held, way = (below, 0) if sign > 0 else (above, 1)
        return pltpu.make_async_remote_copy(
            held[level].at[at], held[level + 1].at[at], s_send.at[level, way, index], s_recv.at[level, way, index],
            device_id=(up if sign > 0 else down, b), device_id_type=MESH)

    hops = [[(hop(level, n, 1), hop(level, n, -1)) for n in range(PIECES)] for level in range(REACH)]

    def on_pair(pair, conditions, act):
        for there, copy in zip(conditions, pair):
            if copy is not None:
                @pl.when(there)
                def _():
                    act(copy)

    def sends(level):
        return (jnp.logical_and(has_up, j >= level), jnp.logical_and(has_down, j < lats - level))

    def send(level, index):
        on_pair(hops[level][index], sends(level), lambda copy: copy.start())

    def receive(level, index):
        on_pair(hops[level][index], (j > level, j < lats - 1 - level), lambda copy: copy.wait_recv())

    lo, hi = pl.ds(0, HALO), pl.ds(HALO + 16, HALO)
    first, last = pl.ds(HALO, HALO), pl.ds(16, HALO)

    def halo(ref, send_sem, recv_sem, rows=None):
        rows = slice(None) if rows is None else rows
        to_east = pltpu.make_async_remote_copy(
            ref.at[rows, last], ref.at[rows, lo], send_sem.at[0], recv_sem.at[0],
            device_id=(j, east), device_id_type=MESH)
        to_west = pltpu.make_async_remote_copy(
            ref.at[rows, first], ref.at[rows, hi], send_sem.at[1], recv_sem.at[1],
            device_id=(j, west), device_id_type=MESH)
        return to_east, to_west

    send(0, 0)
    send(0, 1)
    tables = halo(tab, t_send, t_recv)
    for copy in tables:
        copy.start()
    gathers = []
    for d in range(1, lons):
        copy = pltpu.make_async_remote_copy(
            gath.at[b], gath.at[b], g_send.at[d - 1], g_recv.at[d - 1],
            device_id=(j, lax.rem(b + d, lons)), device_id_type=MESH)
        copy.start()
        gathers.append(copy)
    for n in range(2, PIECES):
        send(0, n)

    for r in range(WIDE + 1, OFF + 1):
        for ref in (xm, l1, r1, l2, r2, l3, r3):
            ref[r + OFF] = zero
            ref[-r + OFF] = zero
    for level in range(REACH):
        for there, ref in ((j > level, below[level + 1]), (j < lats - 1 - level, above[level + 1])):
            @pl.when(jnp.logical_not(there))
            def _():
                @pl.loop(OFF - WIDE, OFF + WIDE + 1)
                def _(n):
                    ref[n] = zero

    @pl.loop(OFF + WIDE + 1, OFF + NLAT - WIDE)
    def _(n):
        out_ref[0, lat_of(n)] = zero

    for copy in gathers:
        copy.wait_recv()
    whole = gath[0]
    for d in range(1, lons):
        whole = whole + gath[d]
    known = {at: whole[n:n + 1] for n, at in enumerate(NEEDED)}

    def turned(value, d):
        return pltpu.roll(value, (-d) % 128, 1) if d else value

    def stencil(step, t):
        u, v, k = known[step, t], known[3 + step, t], known[6, t]
        c_w, c_e = k + jnp.maximum(u, 0.0), k - jnp.minimum(u, 0.0)
        c_s, c_n = k + jnp.maximum(v, 0.0), k - jnp.minimum(v, 0.0)
        return {(0, 0): 1.0 - (c_w + c_e) - (c_s + c_n), (0, -1): c_w, (0, 1): c_e, (-1, 0): c_s, (1, 0): c_n}

    composed = stencil(2, 0)
    for step in (1, 0):
        parts = {}
        for (t, d), weight in composed.items():
            for (dt, dd), value in stencil(step, t).items():
                parts.setdefault((t + dt, d + dd), []).append(weight * turned(value, d))
        composed = {at: functools.reduce(jnp.add, terms) for at, terms in parts.items()}
    slots = {at: n for n, at in enumerate(sorted(composed))}
    for at, n in slots.items():
        taps[n] = jnp.broadcast_to(composed[at], (8, 128))

    def add_rows(a, e, sources, fresh):
        weights = [(t, d, jnp.concatenate([taps[n]] * 2, axis=0)) for (t, d), n in slots.items() if t in sources]

        def run(n, carry):
            total = None if fresh else e0[n, HALO:HALO + 16, :]
            for t in sources:
                center = sources[t][n - t]
                for at, d, weight in weights:
                    if at == t:
                        term = weight * turned(center, d)
                        total = term if total is None else total + term
            e0[n, HALO:HALO + 16, :] = total
            return carry
        lax.fori_loop(a + OFF, e + OFF, run, 0)

    def coefficients(a, e):
        for r in range(a, e):
            at = slice(r + OFF, r + OFF + 1)
            k_r = jnp.broadcast_to(tab[6, :, at], wide_shape)
            for s in range(3):
                u = jnp.broadcast_to(tab[s, :, at], wide_shape)
                v = jnp.broadcast_to(tab[3 + s, :, at], wide_shape)
                c_w, c_e = k_r + jnp.maximum(u, 0.0), k_r - jnp.minimum(u, 0.0)
                c_s, c_n = k_r + jnp.maximum(v, 0.0), k_r - jnp.minimum(v, 0.0)
                co[s, 0, r + OFF] = 1.0 - (c_w + c_e) - (c_s + c_n)
                co[s, 1, r + OFF] = c_w
                co[s, 2, r + OFF] = c_e
                co[s, 3, r + OFF] = c_s
                co[s, 4, r + OFF] = c_n

    def first_step(step, source, store, a, e):
        def run(n, carry):
            center = source[n]
            store(n, co[step, 0, n] * center + co[step, 1, n] * pltpu.roll(center, 1, 0)
                  + co[step, 2, n] * pltpu.roll(center, 2 * HALO + 15, 0)
                  + co[step, 3, n] * source[n - 1] + co[step, 4, n] * source[n + 1])
            return carry
        lax.fori_loop(a + OFF, e + OFF, run, 0)

    def store_1(n, value):
        e1[n] = value

    def store_2(n, value):
        e2[n] = value

    def store_3(n, value):
        out_ref[0, lat_of(n)] = value[HALO:HALO + 16] * keep(n)

    halos = [halo(e0, p_send.at[n], p_recv.at[n], pl.ds(BOUNDS[n] + OFF, BOUNDS[n + 1] - BOUNDS[n]))
             for n in range(PIECES)]
    done = [-18, -17, -16]

    def finish(index):
        for copy in halos[index]:
            copy.wait_recv()
        for step, (source, store) in enumerate(((e0, store_1), (e1, store_2), (e2, store_3))):
            stop = BOUNDS[index + 1] - 1 - step
            first_step(step, source, store, done[step], stop)
            done[step] = stop

    for n in range(PIECES):
        receive(0, n)
        send(1, n)
        if n == 0:
            for copy in tables:
                copy.wait_recv()
            coefficients(-18, -6)
        if n == 1:
            coefficients(-6, 6)
        if n == 2:
            coefficients(6, 19)
    add_rows(-19, 20, {-1: l1, 0: xm, 1: r1}, True)
    for n in range(PIECES):
        receive(1, n)
        send(2, n)
        add_rows(BOUNDS[n] + (1 if n else 0), BOUNDS[n + 1] + (1 if n < PIECES - 1 else 0), {-2: l2}, False)
        add_rows(BOUNDS[n] - (1 if n else 0), BOUNDS[n + 1] - (1 if n < PIECES - 1 else 0), {2: r2}, False)
    for n in range(PIECES):
        receive(2, n)
        add_rows(BOUNDS[n], BOUNDS[n + 1], {-3: l3, 3: r3}, False)
        for copy in halos[n]:
            copy.start()
        if n >= 2:
            finish(n - 2)
    finish(PIECES - 2)
    finish(PIECES - 1)

    for level in range(REACH):
        for n in range(PIECES):
            on_pair(hops[level][n], sends(level), lambda copy: copy.wait_send())
    for copies in halos + [tables] + [gathers]:
        for copy in copies:
            copy.wait_send()


def per_device(covariance, winds, diffusivity, cutoff):
    lats, lons = lax.axis_size("lat"), lax.axis_size("lon")
    vm = lambda *shape: pltpu.VMEM(shape, jnp.float32)
    dma = lambda *shape: pltpu.SemaphoreType.DMA(shape)
    block = (ROWS, 16, 128)
    ext = (ROWS, 16 + 2 * HALO, 128)
    return pl.pallas_call(
        functools.partial(kernel, lats, lons),
        out_shape=jax.ShapeDtypeStruct(covariance.shape, jnp.float32),
        in_specs=[pl.BlockSpec(memory_space=pltpu.HBM)] * 4,
        out_specs=pl.BlockSpec(memory_space=pltpu.VMEM),
        scratch_shapes=[
            pltpu.SMEM((NLAT,), jnp.int32), vm(NLAT, 16, 128), vm(*block), vm(2, 3, 16, NLAT), vm(16, NLAT),
            vm(*block), vm(*block), vm(*block), vm(*block), vm(*block), vm(*block),
            vm(*ext), vm(*ext), vm(*ext), vm(3, 5, *ext), vm(7, 16 + 2 * HALO, 128), vm(lons, PACKED, 128),
            vm(25, 8, 128),
            dma(4), dma(REACH, 2, PIECES), dma(REACH, 2, PIECES), dma(PIECES, 2), dma(PIECES, 2),
            dma(2), dma(2), dma(lons - 1), dma(lons - 1),
        ],
        compiler_params=pltpu.CompilerParams(
            collective_id=0, has_side_effects=True, vmem_limit_bytes=40 * 1024 * 1024),
        cost_estimate=pl.CostEstimate(flops=20_000_000, bytes_accessed=1_500_000, transcendentals=0),
    )(*(pltpu.with_memory_space_constraint(a, pltpu.HBM) for a in (
        covariance, jnp.transpose(winds, (0, 1, 3, 2)), jnp.transpose(diffusivity), cutoff)))


def solution(mesh):
    in_specs = (P("lat", None, "lon", None), P(None, None, None, "lon"), P(None, "lon"), P())
    out_specs = P("lat", None, "lon", None)
    return jax.shard_map(
        per_device, mesh=mesh, in_specs=in_specs, out_specs=out_specs, check_vma=False
    )
```

```python
import functools

import jax
import jax.numpy as jnp
from jax import lax
from jax.experimental import pallas as pl
from jax.experimental.pallas import tpu as pltpu
from jax.sharding import PartitionSpec as P

MESH = pl.DeviceIdType.MESH
NLAT = 64
WIDE = 16
REACH = 3
OFF = 22
ROWS = 2 * OFF + 1
HALO = 8
GROUP = 3
BOUNDS = (-19, -4, 11, 20)
PIECES = len(BOUNDS) - 1
NEEDED = ([(f, t) for f in (0, 3, 6) for t in range(-2, 3)] + [(f, t) for f in (1, 4) for t in range(-1, 2)]
          + [(2, 0), (5, 0)])
PACKED = 24


def piece(index, sign):
    low = max(BOUNDS[index] + sign * REACH, -WIDE)
    high = min(BOUNDS[index + 1] + sign * REACH, WIDE + 1)
    return (low, high) if high > low else None


def kernel(lats, lons, x_ref, winds_ref, diff_ref, cutoff_ref, out_ref,
           cut_ref, xv, xm, wv, dv, l1, r1, l2, r2, l3, r3, e0, e1, e2, co, tab, gath, taps,
           load_sem, s_send, s_recv, p_send, p_recv, t_send, t_recv, g_send, g_recv):
    j = lax.axis_index("lat")
    b = lax.axis_index("lon")
    up, down = lax.rem(j + 1, lats), lax.rem(j + lats - 1, lats)
    east, west = lax.rem(b + 1, lons), lax.rem(b + lons - 1, lons)
    has_up, has_down = j < lats - 1, j > 0

    barrier = pltpu.get_barrier_semaphore()

    @pl.when(has_up)
    def _():
        pl.semaphore_signal(barrier, inc=1, device_id=(up, b), device_id_type=MESH)

    @pl.when(has_down)
    def _():
        pl.semaphore_signal(barrier, inc=1, device_id=(down, b), device_id_type=MESH)

    for d in range(1, lons):
        pl.semaphore_signal(barrier, inc=1, device_id=(j, lax.rem(b + d, lons)), device_id_type=MESH)

    load_x = pltpu.make_async_copy(x_ref.at[0], xv, load_sem.at[0])
    load_w = pltpu.make_async_copy(winds_ref, wv, load_sem.at[1])
    load_d = pltpu.make_async_copy(diff_ref, dv, load_sem.at[2])
    load_c = pltpu.make_async_copy(cutoff_ref, cut_ref, load_sem.at[3])
    load_x.start()
    load_c.start()
    load_w.start()
    load_d.start()

    def lat_of(n):
        return lax.rem(j + n + (NLAT - OFF), NLAT)

    def keep(n):
        cut = cut_ref[lat_of(n)]
        inside = jnp.logical_and(j + n >= OFF, j + n < NLAT + OFF)
        near = jnp.logical_and(n <= OFF + cut, n + cut >= OFF)
        return jnp.where(jnp.logical_and(inside, near), 1.0, 0.0).astype(jnp.float32)

    zero = jnp.zeros((16, 128), jnp.float32)
    wide_shape = (2 * HALO + 16, 128)

    load_c.wait()
    load_x.wait()

    @pl.loop(OFF - WIDE, OFF + WIDE + 1)
    def _(n):
        xm[n] = xv[lat_of(n)] * keep(n)

    inner = jnp.logical_and(has_up, has_down)

    @pl.when(inner)
    def _():
        pl.semaphore_wait(barrier, lons + 1)

    @pl.when(jnp.logical_not(inner))
    def _():
        pl.semaphore_wait(barrier, lons)

    below, above = (xm, l1, l2, l3), (xm, r1, r2, r3)

    def hop(level, index, sign):
        rows = piece(index, sign)
        if rows is None:
            return None
        at = pl.ds(rows[0] + OFF, rows[1] - rows[0])
        held, way = (below, 0) if sign > 0 else (above, 1)
        return pltpu.make_async_remote_copy(
            held[level].at[at], held[level + 1].at[at], s_send.at[level, way, index], s_recv.at[level, way, index],
            device_id=(up if sign > 0 else down, b), device_id_type=MESH)

    hops = [[(hop(level, n, 1), hop(level, n, -1)) for n in range(PIECES)] for level in range(REACH)]

    def on_pair(pair, conditions, act):
        for there, copy in zip(conditions, pair):
            if copy is not None:
                @pl.when(there)
                def _():
                    act(copy)

    def sends(level):
        return (jnp.logical_and(has_up, j >= level), jnp.logical_and(has_down, j < lats - level))

    def send(level, index):
        on_pair(hops[level][index], sends(level), lambda copy: copy.start())

    def receive(level, index):
        on_pair(hops[level][index], (j > level, j < lats - 1 - level), lambda copy: copy.wait_recv())

    lo, hi = pl.ds(0, HALO), pl.ds(HALO + 16, HALO)
    first, last = pl.ds(HALO, HALO), pl.ds(16, HALO)

    def halo(ref, send_sem, recv_sem, rows=None):
        rows = slice(None) if rows is None else rows
        to_east = pltpu.make_async_remote_copy(
            ref.at[rows, last], ref.at[rows, lo], send_sem.at[0], recv_sem.at[0],
            device_id=(j, east), device_id_type=MESH)
        to_west = pltpu.make_async_remote_copy(
            ref.at[rows, first], ref.at[rows, hi], send_sem.at[1], recv_sem.at[1],
            device_id=(j, west), device_id_type=MESH)
        return to_east, to_west

    for n in range(PIECES):
        send(0, n)

    load_w.wait()
    load_d.wait()
    fields = [wv.at[c, s] for c in range(2) for s in range(3)] + [dv]
    lane = lax.broadcasted_iota(jnp.int32, (NLAT, 128), 1)
    sub = lax.broadcasted_iota(jnp.int32, (NLAT, 128), 0)
    turn = jnp.where(lane == sub - j + OFF, 1.0, 0.0).astype(jnp.float32)
    lane = lax.broadcasted_iota(jnp.int32, (16, 128), 1)
    sub = lax.broadcasted_iota(jnp.int32, (16, 128), 0)
    place = jnp.where(lane == sub + b * 16, 1.0, 0.0).astype(jnp.float32)
    tables_own = []
    for n, f in enumerate(fields):
        table = jnp.dot(f[...], turn, precision=lax.Precision.HIGHEST, preferred_element_type=jnp.float32)
        tab[n, HALO:HALO + 16, :] = table
        tables_own.append(table)
    mine = [jnp.sum(tables_own[f][:, OFF + t:OFF + t + 1] * place, axis=0, keepdims=True) for f, t in NEEDED]
    mine += [jnp.zeros((1, 128), jnp.float32)] * (PACKED - len(mine))
    gath[b] = jnp.concatenate(mine, axis=0)

    tables = halo(tab, t_send, t_recv)
    for copy in tables:
        copy.start()
    gathers = []
    for d in range(1, lons):
        copy = pltpu.make_async_remote_copy(
            gath.at[b], gath.at[b], g_send.at[d - 1], g_recv.at[d - 1],
            device_id=(j, lax.rem(b + d, lons)), device_id_type=MESH)
        copy.start()
        gathers.append(copy)

    for r in range(WIDE + 1, OFF + 1):
        for ref in (xm, l1, r1, l2, r2, l3, r3):
            ref[r + OFF] = zero
            ref[-r + OFF] = zero
    for level in range(REACH):
        for there, ref in ((j > level, below[level + 1]), (j < lats - 1 - level, above[level + 1])):
            @pl.when(jnp.logical_not(there))
            def _():
                @pl.loop(OFF - WIDE, OFF + WIDE + 1)
                def _(n):
                    ref[n] = zero

    @pl.loop(OFF + WIDE + 1, OFF + NLAT - WIDE)
    def _(n):
        out_ref[0, lat_of(n)] = zero

    for copy in gathers:
        copy.wait_recv()
    whole = gath[0]
    for d in range(1, lons):
        whole = whole + gath[d]
    known = {at: whole[n:n + 1] for n, at in enumerate(NEEDED)}

    def turned(value, d):
        return pltpu.roll(value, (-d) % 128, value.ndim - 1) if d else value

    def by_groups(a, e, body):
        count = (e - a) // GROUP

        def run(g, carry):
            body(a + OFF + g * GROUP, GROUP)
            return carry
        if count > 1:
            lax.fori_loop(0, count, run, 0)
        elif count:
            body(a + OFF, GROUP)
        if e - a > count * GROUP:
            body(a + OFF + count * GROUP, e - a - count * GROUP)

    def stencil(step, t):
        u, v, k = known[step, t], known[3 + step, t], known[6, t]
        c_w, c_e = k + jnp.maximum(u, 0.0), k - jnp.minimum(u, 0.0)
        c_s, c_n = k + jnp.maximum(v, 0.0), k - jnp.minimum(v, 0.0)
        return {(0, 0): 1.0 - (c_w + c_e) - (c_s + c_n), (0, -1): c_w, (0, 1): c_e, (-1, 0): c_s, (1, 0): c_n}

    composed = stencil(2, 0)
    for step in (1, 0):
        parts = {}
        for (t, d), weight in composed.items():
            for (dt, dd), value in stencil(step, t).items():
                parts.setdefault((t + dt, d + dd), []).append(weight * turned(value, d))
        composed = {at: functools.reduce(jnp.add, terms) for at, terms in parts.items()}
    slots = {at: n for n, at in enumerate(sorted(composed))}
    for at, n in slots.items():
        taps[n] = jnp.broadcast_to(composed[at], (8, 128))

    def add_rows(a, e, sources, fresh):
        weights = [(t, d, jnp.concatenate([taps[n]] * 2, axis=0)) for (t, d), n in slots.items() if t in sources]

        def body(n, count):
            rows = pl.ds(n, count)
            total = None if fresh else e0[rows, HALO:HALO + 16, :]
            for t in sources:
                center = sources[t][pl.ds(n - t, count)]
                for at, d, weight in weights:
                    if at == t:
                        term = weight * turned(center, d)
                        total = term if total is None else total + term
            e0[rows, HALO:HALO + 16, :] = total
        by_groups(a, e, body)

    def coefficients(a, e):
        for r in range(a, e):
            at = slice(r + OFF, r + OFF + 1)
            k_r = jnp.broadcast_to(tab[6, :, at], wide_shape)
            for s in range(3):
                u = jnp.broadcast_to(tab[s, :, at], wide_shape)
                v = jnp.broadcast_to(tab[3 + s, :, at], wide_shape)
                c_w, c_e = k_r + jnp.maximum(u, 0.0), k_r - jnp.minimum(u, 0.0)
                c_s, c_n = k_r + jnp.maximum(v, 0.0), k_r - jnp.minimum(v, 0.0)
                co[s, 0, r + OFF] = 1.0 - (c_w + c_e) - (c_s + c_n)
                co[s, 1, r + OFF] = c_w
                co[s, 2, r + OFF] = c_e
                co[s, 3, r + OFF] = c_s
                co[s, 4, r + OFF] = c_n

    def first_step(step, source, store, a, e):
        def body(n, count):
            rows = pl.ds(n, count)
            center = source[rows]
            store(n, count, co[step, 0, rows] * center + co[step, 1, rows] * pltpu.roll(center, 1, 1)
                  + co[step, 2, rows] * pltpu.roll(center, 2 * HALO + 15, 1)
                  + co[step, 3, rows] * source[pl.ds(n - 1, count)] + co[step, 4, rows] * source[pl.ds(n + 1, count)])
        by_groups(a, e, body)

    def store_1(n, count, value):
        e1[pl.ds(n, count)] = value

    def store_2(n, count, value):
        e2[pl.ds(n, count)] = value

    def store_3(n, count, value):
        for i in range(count):
            out_ref[0, lat_of(n + i)] = value[i, HALO:HALO + 16] * keep(n + i)

    halos = [halo(e0, p_send.at[n], p_recv.at[n], pl.ds(BOUNDS[n] + OFF, BOUNDS[n + 1] - BOUNDS[n]))
             for n in range(PIECES)]
    done = [-18, -17, -16]

    def finish(index):
        for copy in halos[index]:
            copy.wait_recv()
        for step, (source, store) in enumerate(((e0, store_1), (e1, store_2), (e2, store_3))):
            stop = BOUNDS[index + 1] - 1 - step
            first_step(step, source, store, done[step], stop)
            done[step] = stop

    for n in range(PIECES):
        receive(0, n)
        send(1, n)
        if n == 0:
            for copy in tables:
                copy.wait_recv()
            coefficients(-18, -6)
        if n == 1:
            coefficients(-6, 6)
        if n == 2:
            coefficients(6, 19)
    add_rows(-19, 20, {-1: l1, 0: xm, 1: r1}, True)
    for n in range(PIECES):
        receive(1, n)
        send(2, n)
        add_rows(BOUNDS[n] + (1 if n else 0), BOUNDS[n + 1] + (1 if n < PIECES - 1 else 0), {-2: l2}, False)
        add_rows(BOUNDS[n] - (1 if n else 0), BOUNDS[n + 1] - (1 if n < PIECES - 1 else 0), {2: r2}, False)
    for n in range(PIECES):
        receive(2, n)
        add_rows(BOUNDS[n], BOUNDS[n + 1], {-3: l3, 3: r3}, False)
        for copy in halos[n]:
            copy.start()
        if n >= 2:
            finish(n - 2)
    finish(PIECES - 2)
    finish(PIECES - 1)

    for level in range(REACH):
        for n in range(PIECES):
            on_pair(hops[level][n], sends(level), lambda copy: copy.wait_send())
    for copies in halos + [tables] + [gathers]:
        for copy in copies:
            copy.wait_send()


def per_device(covariance, winds, diffusivity, cutoff):
    lats, lons = lax.axis_size("lat"), lax.axis_size("lon")
    vm = lambda *shape: pltpu.VMEM(shape, jnp.float32)
    dma = lambda *shape: pltpu.SemaphoreType.DMA(shape)
    block = (ROWS, 16, 128)
    ext = (ROWS, 16 + 2 * HALO, 128)
    return pl.pallas_call(
        functools.partial(kernel, lats, lons),
        out_shape=jax.ShapeDtypeStruct(covariance.shape, jnp.float32),
        in_specs=[pl.BlockSpec(memory_space=pltpu.HBM)] * 4,
        out_specs=pl.BlockSpec(memory_space=pltpu.VMEM),
        scratch_shapes=[
            pltpu.SMEM((NLAT,), jnp.int32), vm(NLAT, 16, 128), vm(*block), vm(2, 3, 16, NLAT), vm(16, NLAT),
            vm(*block), vm(*block), vm(*block), vm(*block), vm(*block), vm(*block),
            vm(*ext), vm(*ext), vm(*ext), vm(3, 5, *ext), vm(7, 16 + 2 * HALO, 128), vm(lons, PACKED, 128),
            vm(25, 8, 128),
            dma(4), dma(REACH, 2, PIECES), dma(REACH, 2, PIECES), dma(PIECES, 2), dma(PIECES, 2),
            dma(2), dma(2), dma(lons - 1), dma(lons - 1),
        ],
        compiler_params=pltpu.CompilerParams(
            collective_id=0, has_side_effects=True, vmem_limit_bytes=40 * 1024 * 1024),
        cost_estimate=pl.CostEstimate(flops=20_000_000, bytes_accessed=1_500_000, transcendentals=0),
    )(*(pltpu.with_memory_space_constraint(a, pltpu.HBM) for a in (
        covariance, jnp.transpose(winds, (0, 1, 3, 2)), jnp.transpose(diffusivity), cutoff)))


def solution(mesh):
    in_specs = (P("lat", None, "lon", None), P(None, None, None, "lon"), P(None, "lon"), P())
    out_specs = P("lat", None, "lon", None)
    return jax.shard_map(
        per_device, mesh=mesh, in_specs=in_specs, out_specs=out_specs, check_vma=False
    )
```

```python
import functools

import jax
import jax.numpy as jnp
from jax import lax
from jax.experimental import pallas as pl
from jax.experimental.pallas import tpu as pltpu
from jax.sharding import PartitionSpec as P

MESH = pl.DeviceIdType.MESH
NLAT = 64
WIDE = 16
REACH = 3
OFF = 22
ROWS = 2 * OFF + 1
HALO = 8
GROUP = 6
BOUNDS = (-19, -4, 11, 20)
PIECES = len(BOUNDS) - 1
NEEDED = ([(f, t) for f in (0, 3, 6) for t in range(-2, 3)] + [(f, t) for f in (1, 4) for t in range(-1, 2)]
          + [(2, 0), (5, 0)])
PACKED = 24


def piece(index, sign):
    low = max(BOUNDS[index] + sign * REACH, -WIDE)
    high = min(BOUNDS[index + 1] + sign * REACH, WIDE + 1)
    return (low, high) if high > low else None


def kernel(lats, lons, x_ref, winds_ref, diff_ref, cutoff_ref, out_ref,
           cut_ref, xv, xm, wv, dv, l1, r1, l2, r2, l3, r3, e0, e1, e2, co, tab, gath, taps,
           load_sem, s_send, s_recv, p_send, p_recv, t_send, t_recv, g_send, g_recv):
    j = lax.axis_index("lat")
    b = lax.axis_index("lon")
    up, down = lax.rem(j + 1, lats), lax.rem(j + lats - 1, lats)
    east, west = lax.rem(b + 1, lons), lax.rem(b + lons - 1, lons)
    has_up, has_down = j < lats - 1, j > 0

    barrier = pltpu.get_barrier_semaphore()

    @pl.when(has_up)
    def _():
        pl.semaphore_signal(barrier, inc=1, device_id=(up, b), device_id_type=MESH)

    @pl.when(has_down)
    def _():
        pl.semaphore_signal(barrier, inc=1, device_id=(down, b), device_id_type=MESH)

    for d in range(1, lons):
        pl.semaphore_signal(barrier, inc=1, device_id=(j, lax.rem(b + d, lons)), device_id_type=MESH)

    load_x = pltpu.make_async_copy(x_ref.at[0], xv, load_sem.at[0])
    load_w = pltpu.make_async_copy(winds_ref, wv, load_sem.at[1])
    load_d = pltpu.make_async_copy(diff_ref, dv, load_sem.at[2])
    load_c = pltpu.make_async_copy(cutoff_ref, cut_ref, load_sem.at[3])
    load_x.start()
    load_c.start()
    load_w.start()
    load_d.start()

    def lat_of(n):
        return lax.rem(j + n + (NLAT - OFF), NLAT)

    def keep(n):
        cut = cut_ref[lat_of(n)]
        inside = jnp.logical_and(j + n >= OFF, j + n < NLAT + OFF)
        near = jnp.logical_and(n <= OFF + cut, n + cut >= OFF)
        return jnp.where(jnp.logical_and(inside, near), 1.0, 0.0).astype(jnp.float32)

    zero = jnp.zeros((16, 128), jnp.float32)
    wide_shape = (2 * HALO + 16, 128)

    load_c.wait()
    load_x.wait()

    @pl.loop(0, 11)
    def _(g):
        for i in range(3):
            n = OFF - WIDE + 3 * g + i
            xm[n] = xv[lat_of(n)] * keep(n)

    inner = jnp.logical_and(has_up, has_down)

    @pl.when(inner)
    def _():
        pl.semaphore_wait(barrier, lons + 1)

    @pl.when(jnp.logical_not(inner))
    def _():
        pl.semaphore_wait(barrier, lons)

    below, above = (xm, l1, l2, l3), (xm, r1, r2, r3)

    def hop(level, index, sign):
        rows = piece(index, sign)
        if rows is None:
            return None
        at = pl.ds(rows[0] + OFF, rows[1] - rows[0])
        held, way = (below, 0) if sign > 0 else (above, 1)
        return pltpu.make_async_remote_copy(
            held[level].at[at], held[level + 1].at[at], s_send.at[level, way, index], s_recv.at[level, way, index],
            device_id=(up if sign > 0 else down, b), device_id_type=MESH)

    hops = [[(hop(level, n, 1), hop(level, n, -1)) for n in range(PIECES)] for level in range(REACH)]

    def on_pair(pair, conditions, act):
        for there, copy in zip(conditions, pair):
            if copy is not None:
                @pl.when(there)
                def _():
                    act(copy)

    def sends(level):
        return (jnp.logical_and(has_up, j >= level), jnp.logical_and(has_down, j < lats - level))

    def send(level, index):
        on_pair(hops[level][index], sends(level), lambda copy: copy.start())

    def receive(level, index):
        on_pair(hops[level][index], (j > level, j < lats - 1 - level), lambda copy: copy.wait_recv())

    def forward(level, index):
        for side in (0, 1):
            come, go = hops[level][index][side], hops[level + 1][index][side]
            if come is not None:
                arrives = (j > level, j < lats - 1 - level)[side]
                goes = sends(level + 1)[side]

                @pl.when(arrives)
                def _():
                    come.wait_recv()

                @pl.when(goes)
                def _():
                    go.start()

    lo, hi = pl.ds(0, HALO), pl.ds(HALO + 16, HALO)
    first, last = pl.ds(HALO, HALO), pl.ds(16, HALO)

    def halo(ref, send_sem, recv_sem, rows=None):
        rows = slice(None) if rows is None else rows
        to_east = pltpu.make_async_remote_copy(
            ref.at[rows, last], ref.at[rows, lo], send_sem.at[0], recv_sem.at[0],
            device_id=(j, east), device_id_type=MESH)
        to_west = pltpu.make_async_remote_copy(
            ref.at[rows, first], ref.at[rows, hi], send_sem.at[1], recv_sem.at[1],
            device_id=(j, west), device_id_type=MESH)
        return to_east, to_west

    for n in range(PIECES):
        send(0, n)

    load_w.wait()
    load_d.wait()
    fields = [wv.at[c, s] for c in range(2) for s in range(3)] + [dv]
    lane = lax.broadcasted_iota(jnp.int32, (NLAT, 128), 1)
    sub = lax.broadcasted_iota(jnp.int32, (NLAT, 128), 0)
    turn = jnp.where(lane == sub - j + OFF, 1.0, 0.0).astype(jnp.float32)
    lane = lax.broadcasted_iota(jnp.int32, (16, 128), 1)
    sub = lax.broadcasted_iota(jnp.int32, (16, 128), 0)
    place = jnp.where(lane == sub + b * 16, 1.0, 0.0).astype(jnp.float32)
    tables_own = []
    for n, f in enumerate(fields):
        table = jnp.dot(f[...], turn, precision=lax.Precision.HIGHEST, preferred_element_type=jnp.float32)
        tab[n, HALO:HALO + 16, :] = table
        tables_own.append(table)
    mine = [jnp.sum(tables_own[f][:, OFF + t:OFF + t + 1] * place, axis=0, keepdims=True) for f, t in NEEDED]
    mine += [jnp.zeros((1, 128), jnp.float32)] * (PACKED - len(mine))
    gath[b] = jnp.concatenate(mine, axis=0)

    tables = halo(tab, t_send, t_recv)
    for copy in tables:
        copy.start()
    gathers = []
    for d in range(1, lons):
        copy = pltpu.make_async_remote_copy(
            gath.at[b], gath.at[b], g_send.at[d - 1], g_recv.at[d - 1],
            device_id=(j, lax.rem(b + d, lons)), device_id_type=MESH)
        copy.start()
        gathers.append(copy)

    for r in range(WIDE + 1, OFF + 1):
        for ref in (xm, l1, r1, l2, r2, l3, r3):
            ref[r + OFF] = zero
            ref[-r + OFF] = zero
    for level in range(REACH):
        for there, ref in ((j > level, below[level + 1]), (j < lats - 1 - level, above[level + 1])):
            @pl.when(jnp.logical_not(there))
            def _():
                @pl.loop(OFF - WIDE, OFF + WIDE + 1)
                def _(n):
                    ref[n] = zero

    @pl.loop(OFF + WIDE + 1, OFF + NLAT - WIDE)
    def _(n):
        out_ref[0, lat_of(n)] = zero

    for copy in gathers:
        copy.wait_recv()
    whole = gath[0]
    for d in range(1, lons):
        whole = whole + gath[d]
    known = {at: whole[n:n + 1] for n, at in enumerate(NEEDED)}

    def turned(value, d):
        return pltpu.roll(value, (-d) % 128, value.ndim - 1) if d else value

    def by_groups(a, e, body):
        count = (e - a) // GROUP

        def run(g, carry):
            body(a + OFF + g * GROUP, GROUP)
            return carry
        if count > 1:
            lax.fori_loop(0, count, run, 0)
        elif count:
            body(a + OFF, GROUP)
        if e - a > count * GROUP:
            body(a + OFF + count * GROUP, e - a - count * GROUP)

    def stencil(step, t):
        u, v, k = known[step, t], known[3 + step, t], known[6, t]
        c_w, c_e = k + jnp.maximum(u, 0.0), k - jnp.minimum(u, 0.0)
        c_s, c_n = k + jnp.maximum(v, 0.0), k - jnp.minimum(v, 0.0)
        return {(0, 0): 1.0 - (c_w + c_e) - (c_s + c_n), (0, -1): c_w, (0, 1): c_e, (-1, 0): c_s, (1, 0): c_n}

    composed = stencil(2, 0)
    for step in (1, 0):
        parts = {}
        for (t, d), weight in composed.items():
            for (dt, dd), value in stencil(step, t).items():
                parts.setdefault((t + dt, d + dd), []).append(weight * turned(value, d))
        composed = {at: functools.reduce(jnp.add, terms) for at, terms in parts.items()}
    slots = {at: n for n, at in enumerate(sorted(composed))}
    for at, n in slots.items():
        taps[n] = jnp.broadcast_to(composed[at], (8, 128))

    def add_rows(a, e, sources, fresh):
        weights = [(t, d, jnp.concatenate([taps[n]] * 2, axis=0)) for (t, d), n in slots.items() if t in sources]

        def body(n, count):
            rows = pl.ds(n, count)
            total = None if fresh else e0[rows, HALO:HALO + 16, :]
            for t in sources:
                center = sources[t][pl.ds(n - t, count)]
                for at, d, weight in weights:
                    if at == t:
                        term = weight * turned(center, d)
                        total = term if total is None else total + term
            e0[rows, HALO:HALO + 16, :] = total
        by_groups(a, e, body)

    def coefficients(a, e):
        for r in range(a, e):
            at = slice(r + OFF, r + OFF + 1)
            k_r = jnp.broadcast_to(tab[6, :, at], wide_shape)
            for s in range(3):
                u = jnp.broadcast_to(tab[s, :, at], wide_shape)
                v = jnp.broadcast_to(tab[3 + s, :, at], wide_shape)
                c_w, c_e = k_r + jnp.maximum(u, 0.0), k_r - jnp.minimum(u, 0.0)
                c_s, c_n = k_r + jnp.maximum(v, 0.0), k_r - jnp.minimum(v, 0.0)
                co[s, 0, r + OFF] = 1.0 - (c_w + c_e) - (c_s + c_n)
                co[s, 1, r + OFF] = c_w
                co[s, 2, r + OFF] = c_e
                co[s, 3, r + OFF] = c_s
                co[s, 4, r + OFF] = c_n

    def first_step(step, source, store, a, e):
        def body(n, count):
            rows = pl.ds(n, count)
            center = source[rows]
            store(n, count, co[step, 0, rows] * center + co[step, 1, rows] * pltpu.roll(center, 1, 1)
                  + co[step, 2, rows] * pltpu.roll(center, 2 * HALO + 15, 1)
                  + co[step, 3, rows] * source[pl.ds(n - 1, count)] + co[step, 4, rows] * source[pl.ds(n + 1, count)])
        by_groups(a, e, body)

    def store_1(n, count, value):
        e1[pl.ds(n, count)] = value

    def store_2(n, count, value):
        e2[pl.ds(n, count)] = value

    def store_3(n, count, value):
        for i in range(count):
            out_ref[0, lat_of(n + i)] = value[i, HALO:HALO + 16] * keep(n + i)

    halos = [halo(e0, p_send.at[n], p_recv.at[n], pl.ds(BOUNDS[n] + OFF, BOUNDS[n + 1] - BOUNDS[n]))
             for n in range(PIECES)]
    done = [-18, -17, -16]

    def finish(index):
        for copy in halos[index]:
            copy.wait_recv()
        for step, (source, store) in enumerate(((e0, store_1), (e1, store_2), (e2, store_3))):
            stop = BOUNDS[index + 1] - 1 - step
            first_step(step, source, store, done[step], stop)
            done[step] = stop

    for n in range(PIECES):
        forward(0, n)
        if n == 0:
            for copy in tables:
                copy.wait_recv()
            coefficients(-18, -6)
        if n == 1:
            coefficients(-6, 6)
        if n == 2:
            coefficients(6, 19)
    add_rows(-19, 20, {-1: l1, 0: xm, 1: r1}, True)
    for n in range(PIECES):
        forward(1, n)
        add_rows(BOUNDS[n] + (1 if n else 0), BOUNDS[n + 1] + (1 if n < PIECES - 1 else 0), {-2: l2}, False)
        add_rows(BOUNDS[n] - (1 if n else 0), BOUNDS[n + 1] - (1 if n < PIECES - 1 else 0), {2: r2}, False)
    for n in range(PIECES):
        receive(2, n)
        add_rows(BOUNDS[n], BOUNDS[n + 1], {-3: l3, 3: r3}, False)
        for copy in halos[n]:
            copy.start()
        if n >= 2:
            finish(n - 2)
    finish(PIECES - 2)
    finish(PIECES - 1)

    for level in range(REACH):
        for n in range(PIECES):
            on_pair(hops[level][n], sends(level), lambda copy: copy.wait_send())
    for copies in halos + [tables] + [gathers]:
        for copy in copies:
            copy.wait_send()


def per_device(covariance, winds, diffusivity, cutoff):
    lats, lons = lax.axis_size("lat"), lax.axis_size("lon")
    vm = lambda *shape: pltpu.VMEM(shape, jnp.float32)
    dma = lambda *shape: pltpu.SemaphoreType.DMA(shape)
    block = (ROWS, 16, 128)
    ext = (ROWS, 16 + 2 * HALO, 128)
    return pl.pallas_call(
        functools.partial(kernel, lats, lons),
        out_shape=jax.ShapeDtypeStruct(covariance.shape, jnp.float32),
        in_specs=[pl.BlockSpec(memory_space=pltpu.HBM)] * 4,
        out_specs=pl.BlockSpec(memory_space=pltpu.VMEM),
        scratch_shapes=[
            pltpu.SMEM((NLAT,), jnp.int32), vm(NLAT, 16, 128), vm(*block), vm(2, 3, 16, NLAT), vm(16, NLAT),
            vm(*block), vm(*block), vm(*block), vm(*block), vm(*block), vm(*block),
            vm(*ext), vm(*ext), vm(*ext), vm(3, 5, *ext), vm(7, 16 + 2 * HALO, 128), vm(lons, PACKED, 128),
            vm(25, 8, 128),
            dma(4), dma(REACH, 2, PIECES), dma(REACH, 2, PIECES), dma(PIECES, 2), dma(PIECES, 2),
            dma(2), dma(2), dma(lons - 1), dma(lons - 1),
        ],
        compiler_params=pltpu.CompilerParams(
            collective_id=0, has_side_effects=True, vmem_limit_bytes=40 * 1024 * 1024),
        cost_estimate=pl.CostEstimate(flops=20_000_000, bytes_accessed=1_500_000, transcendentals=0),
    )(*(pltpu.with_memory_space_constraint(a, pltpu.HBM) for a in (
        covariance, jnp.transpose(winds, (0, 1, 3, 2)), jnp.transpose(diffusivity), cutoff)))


def solution(mesh):
    in_specs = (P("lat", None, "lon", None), P(None, None, None, "lon"), P(None, "lon"), P())
    out_specs = P("lat", None, "lon", None)
    return jax.shard_map(
        per_device, mesh=mesh, in_specs=in_specs, out_specs=out_specs, check_vma=False
    )
```

```python
import functools

import jax
import jax.numpy as jnp
from jax import lax
from jax.experimental import pallas as pl
from jax.experimental.pallas import tpu as pltpu
from jax.sharding import PartitionSpec as P

MESH = pl.DeviceIdType.MESH
NLAT = 64
WIDE = 16
REACH = 3
OFF = 22
ROWS = 2 * OFF + 1
HALO = 8
GROUP = 6
BOUNDS = (-19, -6, 9, 20)
PIECES = len(BOUNDS) - 1
NEEDED = ([(f, t) for f in (0, 3, 6) for t in range(-2, 3)] + [(f, t) for f in (1, 4) for t in range(-1, 2)]
          + [(2, 0), (5, 0)])
PACKED = 24


def piece(index, sign):
    low = max(BOUNDS[index] + sign * REACH, -WIDE)
    high = min(BOUNDS[index + 1] + sign * REACH, WIDE + 1)
    return (low, high) if high > low else None


def kernel(lats, lons, x_ref, winds_ref, diff_ref, cutoff_ref, out_ref,
           cut_ref, xv, xm, wv, dv, l1, r1, l2, r2, l3, r3, e0, e1, e2, co, tab, gath, taps,
           load_sem, s_send, s_recv, p_send, p_recv, t_send, t_recv, g_send, g_recv):
    j = lax.axis_index("lat")
    b = lax.axis_index("lon")
    up, down = lax.rem(j + 1, lats), lax.rem(j + lats - 1, lats)
    east, west = lax.rem(b + 1, lons), lax.rem(b + lons - 1, lons)
    has_up, has_down = j < lats - 1, j > 0

    barrier = pltpu.get_barrier_semaphore()

    @pl.when(has_up)
    def _():
        pl.semaphore_signal(barrier, inc=1, device_id=(up, b), device_id_type=MESH)

    @pl.when(has_down)
    def _():
        pl.semaphore_signal(barrier, inc=1, device_id=(down, b), device_id_type=MESH)

    for d in range(1, lons):
        pl.semaphore_signal(barrier, inc=1, device_id=(j, lax.rem(b + d, lons)), device_id_type=MESH)

    load_x = pltpu.make_async_copy(x_ref.at[0], xv, load_sem.at[0])
    load_w = pltpu.make_async_copy(winds_ref, wv, load_sem.at[1])
    load_d = pltpu.make_async_copy(diff_ref, dv, load_sem.at[2])
    load_c = pltpu.make_async_copy(cutoff_ref, cut_ref, load_sem.at[3])
    load_x.start()
    load_c.start()
    load_w.start()
    load_d.start()

    def lat_of(n):
        return lax.rem(j + n + (NLAT - OFF), NLAT)

    def keep(n):
        cut = cut_ref[lat_of(n)]
        inside = jnp.logical_and(j + n >= OFF, j + n < NLAT + OFF)
        near = jnp.logical_and(n <= OFF + cut, n + cut >= OFF)
        return jnp.where(jnp.logical_and(inside, near), 1.0, 0.0).astype(jnp.float32)

    zero = jnp.zeros((16, 128), jnp.float32)
    wide_shape = (2 * HALO + 16, 128)

    load_c.wait()
    load_x.wait()

    @pl.loop(0, 11)
    def _(g):
        for i in range(3):
            n = OFF - WIDE + 3 * g + i
            xm[n] = xv[lat_of(n)] * keep(n)

    inner = jnp.logical_and(has_up, has_down)

    @pl.when(inner)
    def _():
        pl.semaphore_wait(barrier, lons + 1)

    @pl.when(jnp.logical_not(inner))
    def _():
        pl.semaphore_wait(barrier, lons)

    below, above = (xm, l1, l2, l3), (xm, r1, r2, r3)

    def hop(level, index, sign):
        rows = piece(index, sign)
        if rows is None:
            return None
        at = pl.ds(rows[0] + OFF, rows[1] - rows[0])
        held, way = (below, 0) if sign > 0 else (above, 1)
        return pltpu.make_async_remote_copy(
            held[level].at[at], held[level + 1].at[at], s_send.at[level, way, index], s_recv.at[level, way, index],
            device_id=(up if sign > 0 else down, b), device_id_type=MESH)

    hops = [[(hop(level, n, 1), hop(level, n, -1)) for n in range(PIECES)] for level in range(REACH)]

    def on_pair(pair, conditions, act):
        for there, copy in zip(conditions, pair):
            if copy is not None:
                @pl.when(there)
                def _():
                    act(copy)

    def sends(level):
        return (jnp.logical_and(has_up, j >= level), jnp.logical_and(has_down, j < lats - level))

    def send(level, index):
        on_pair(hops[level][index], sends(level), lambda copy: copy.start())

    def receive(level, index):
        on_pair(hops[level][index], (j > level, j < lats - 1 - level), lambda copy: copy.wait_recv())

    def forward(level, index, sides=(0, 1), when=True):
        for side in sides:
            come, go = hops[level][index][side], hops[level + 1][index][side]
            if come is not None:
                arrives = (j > level, j < lats - 1 - level)[side]
                goes = sends(level + 1)[side]

                @pl.when(jnp.logical_and(arrives, when))
                def _():
                    come.wait_recv()

                @pl.when(jnp.logical_and(goes, when))
                def _():
                    go.start()

    lo, hi = pl.ds(0, HALO), pl.ds(HALO + 16, HALO)
    first, last = pl.ds(HALO, HALO), pl.ds(16, HALO)

    def halo(ref, send_sem, recv_sem, rows=None):
        rows = slice(None) if rows is None else rows
        to_east = pltpu.make_async_remote_copy(
            ref.at[rows, last], ref.at[rows, lo], send_sem.at[0], recv_sem.at[0],
            device_id=(j, east), device_id_type=MESH)
        to_west = pltpu.make_async_remote_copy(
            ref.at[rows, first], ref.at[rows, hi], send_sem.at[1], recv_sem.at[1],
            device_id=(j, west), device_id_type=MESH)
        return to_east, to_west

    for n in range(PIECES):
        send(0, n)

    load_w.wait()
    load_d.wait()
    fields = [wv.at[c, s] for c in range(2) for s in range(3)] + [dv]
    lane = lax.broadcasted_iota(jnp.int32, (NLAT, 128), 1)
    sub = lax.broadcasted_iota(jnp.int32, (NLAT, 128), 0)
    turn = jnp.where(lane == sub - j + OFF, 1.0, 0.0).astype(jnp.float32)
    lane = lax.broadcasted_iota(jnp.int32, (16, 128), 1)
    sub = lax.broadcasted_iota(jnp.int32, (16, 128), 0)
    place = jnp.where(lane == sub + b * 16, 1.0, 0.0).astype(jnp.float32)
    tables_own = []
    for n, f in enumerate(fields):
        table = jnp.dot(f[...], turn, precision=lax.Precision.HIGHEST, preferred_element_type=jnp.float32)
        tab[n, HALO:HALO + 16, :] = table
        tables_own.append(table)
    mine = [jnp.sum(tables_own[f][:, OFF + t:OFF + t + 1] * place, axis=0, keepdims=True) for f, t in NEEDED]
    mine += [jnp.zeros((1, 128), jnp.float32)] * (PACKED - len(mine))
    gath[b] = jnp.concatenate(mine, axis=0)

    tables = halo(tab, t_send, t_recv)
    for copy in tables:
        copy.start()
    gathers = []
    for d in range(1, lons):
        copy = pltpu.make_async_remote_copy(
            gath.at[b], gath.at[b], g_send.at[d - 1], g_recv.at[d - 1],
            device_id=(j, lax.rem(b + d, lons)), device_id_type=MESH)
        copy.start()
        gathers.append(copy)

    for r in range(WIDE + 1, OFF + 1):
        for ref in (xm, l1, r1, l2, r2, l3, r3):
            ref[r + OFF] = zero
            ref[-r + OFF] = zero
    for level in range(REACH):
        for there, ref in ((j > level, below[level + 1]), (j < lats - 1 - level, above[level + 1])):
            @pl.when(jnp.logical_not(there))
            def _():
                @pl.loop(OFF - WIDE, OFF + WIDE + 1)
                def _(n):
                    ref[n] = zero

    @pl.loop(OFF + WIDE + 1, OFF + NLAT - WIDE)
    def _(n):
        out_ref[0, lat_of(n)] = zero

    for copy in gathers:
        copy.wait_recv()
    whole = gath[0]
    for d in range(1, lons):
        whole = whole + gath[d]
    known = {at: whole[n:n + 1] for n, at in enumerate(NEEDED)}

    def turned(value, d):
        return pltpu.roll(value, (-d) % 128, value.ndim - 1) if d else value

    def by_groups(a, e, body):
        count = (e - a) // GROUP

        def run(g, carry):
            body(a + OFF + g * GROUP, GROUP)
            return carry
        if count > 1:
            lax.fori_loop(0, count, run, 0)
        elif count:
            body(a + OFF, GROUP)
        if e - a > count * GROUP:
            body(a + OFF + count * GROUP, e - a - count * GROUP)

    def stencil(step, t):
        u, v, k = known[step, t], known[3 + step, t], known[6, t]
        c_w, c_e = k + jnp.maximum(u, 0.0), k - jnp.minimum(u, 0.0)
        c_s, c_n = k + jnp.maximum(v, 0.0), k - jnp.minimum(v, 0.0)
        return {(0, 0): 1.0 - (c_w + c_e) - (c_s + c_n), (0, -1): c_w, (0, 1): c_e, (-1, 0): c_s, (1, 0): c_n}

    composed = stencil(2, 0)
    for step in (1, 0):
        parts = {}
        for (t, d), weight in composed.items():
            for (dt, dd), value in stencil(step, t).items():
                parts.setdefault((t + dt, d + dd), []).append(weight * turned(value, d))
        composed = {at: functools.reduce(jnp.add, terms) for at, terms in parts.items()}
    slots = {at: n for n, at in enumerate(sorted(composed))}
    for at, n in slots.items():
        taps[n] = jnp.broadcast_to(composed[at], (8, 128))

    def add_rows(a, e, sources, fresh):
        weights = [(t, d, jnp.concatenate([taps[n]] * 2, axis=0)) for (t, d), n in slots.items() if t in sources]

        def body(n, count):
            rows = pl.ds(n, count)
            total = None if fresh else e0[rows, HALO:HALO + 16, :]
            for t in sources:
                center = sources[t][pl.ds(n - t, count)]
                for at, d, weight in weights:
                    if at == t:
                        term = weight * turned(center, d)
                        total = term if total is None else total + term
            e0[rows, HALO:HALO + 16, :] = total
        by_groups(a, e, body)

    def coefficients(a, e):
        for r in range(a, e):
            at = slice(r + OFF, r + OFF + 1)
            k_r = jnp.broadcast_to(tab[6, :, at], wide_shape)
            for s in range(3):
                u = jnp.broadcast_to(tab[s, :, at], wide_shape)
                v = jnp.broadcast_to(tab[3 + s, :, at], wide_shape)
                c_w, c_e = k_r + jnp.maximum(u, 0.0), k_r - jnp.minimum(u, 0.0)
                c_s, c_n = k_r + jnp.maximum(v, 0.0), k_r - jnp.minimum(v, 0.0)
                co[s, 0, r + OFF] = 1.0 - (c_w + c_e) - (c_s + c_n)
                co[s, 1, r + OFF] = c_w
                co[s, 2, r + OFF] = c_e
                co[s, 3, r + OFF] = c_s
                co[s, 4, r + OFF] = c_n

    def first_step(step, source, store, a, e):
        def body(n, count):
            rows = pl.ds(n, count)
            center = source[rows]
            store(n, count, co[step, 0, rows] * center + co[step, 1, rows] * pltpu.roll(center, 1, 1)
                  + co[step, 2, rows] * pltpu.roll(center, 2 * HALO + 15, 1)
                  + co[step, 3, rows] * source[pl.ds(n - 1, count)] + co[step, 4, rows] * source[pl.ds(n + 1, count)])
        by_groups(a, e, body)

    def store_1(n, count, value):
        e1[pl.ds(n, count)] = value

    def store_2(n, count, value):
        e2[pl.ds(n, count)] = value

    def store_3(n, count, value):
        for i in range(count):
            out_ref[0, lat_of(n + i)] = value[i, HALO:HALO + 16] * keep(n + i)

    halos = [halo(e0, p_send.at[n], p_recv.at[n], pl.ds(BOUNDS[n] + OFF, BOUNDS[n + 1] - BOUNDS[n]))
             for n in range(PIECES)]
    done = [-18, -17, -16]

    def finish(index):
        for copy in halos[index]:
            copy.wait_recv()
        for step, (source, store) in enumerate(((e0, store_1), (e1, store_2), (e2, store_3))):
            stop = BOUNDS[index + 1] - 1 - step
            first_step(step, source, store, done[step], stop)
            done[step] = stop

    for n in range(PIECES):
        forward(0, n)
        if n == 0:
            for copy in tables:
                copy.wait_recv()
            coefficients(-18, -6)
        if n == 1:
            coefficients(-6, 6)
        if n == 2:
            coefficients(6, 19)
    add_rows(-19, 20, {-1: l1, 0: xm, 1: r1}, True)
    early = lax.rem(j, 16) == 0
    for n in range(PIECES):
        forward(1, n, (1,), early)
    for n in range(PIECES):
        forward(1, n, (0,))
        forward(1, n, (1,), jnp.logical_not(early))
        add_rows(BOUNDS[n] + (1 if n else 0), BOUNDS[n + 1] + (1 if n < PIECES - 1 else 0), {-2: l2}, False)
        add_rows(BOUNDS[n] - (1 if n else 0), BOUNDS[n + 1] - (1 if n < PIECES - 1 else 0), {2: r2}, False)
    for n in range(PIECES):
        receive(2, n)
        add_rows(BOUNDS[n], BOUNDS[n + 1], {-3: l3, 3: r3}, False)
        for copy in halos[n]:
            copy.start()
        if n >= 2:
            finish(n - 2)
    finish(PIECES - 2)
    finish(PIECES - 1)

    for level in range(REACH):
        for n in range(PIECES):
            on_pair(hops[level][n], sends(level), lambda copy: copy.wait_send())
    for copies in halos + [tables] + [gathers]:
        for copy in copies:
            copy.wait_send()


def per_device(covariance, winds, diffusivity, cutoff):
    lats, lons = lax.axis_size("lat"), lax.axis_size("lon")
    vm = lambda *shape: pltpu.VMEM(shape, jnp.float32)
    dma = lambda *shape: pltpu.SemaphoreType.DMA(shape)
    block = (ROWS, 16, 128)
    ext = (ROWS, 16 + 2 * HALO, 128)
    return pl.pallas_call(
        functools.partial(kernel, lats, lons),
        out_shape=jax.ShapeDtypeStruct(covariance.shape, jnp.float32),
        in_specs=[pl.BlockSpec(memory_space=pltpu.HBM)] * 4,
        out_specs=pl.BlockSpec(memory_space=pltpu.VMEM),
        scratch_shapes=[
            pltpu.SMEM((NLAT,), jnp.int32), vm(NLAT, 16, 128), vm(*block), vm(2, 3, 16, NLAT), vm(16, NLAT),
            vm(*block), vm(*block), vm(*block), vm(*block), vm(*block), vm(*block),
            vm(*ext), vm(*ext), vm(*ext), vm(3, 5, *ext), vm(7, 16 + 2 * HALO, 128), vm(lons, PACKED, 128),
            vm(25, 8, 128),
            dma(4), dma(REACH, 2, PIECES), dma(REACH, 2, PIECES), dma(PIECES, 2), dma(PIECES, 2),
            dma(2), dma(2), dma(lons - 1), dma(lons - 1),
        ],
        compiler_params=pltpu.CompilerParams(
            collective_id=0, has_side_effects=True, vmem_limit_bytes=40 * 1024 * 1024),
        cost_estimate=pl.CostEstimate(flops=20_000_000, bytes_accessed=1_500_000, transcendentals=0),
    )(*(pltpu.with_memory_space_constraint(a, pltpu.HBM) for a in (
        covariance, jnp.transpose(winds, (0, 1, 3, 2)), jnp.transpose(diffusivity), cutoff)))


def solution(mesh):
    in_specs = (P("lat", None, "lon", None), P(None, None, None, "lon"), P(None, "lon"), P())
    out_specs = P("lat", None, "lon", None)
    return jax.shard_map(
        per_device, mesh=mesh, in_specs=in_specs, out_specs=out_specs, check_vma=False
    )
```
